256 devices in a mesh: dp: 32 (over y, z_lo, core), tensor: 8 (over x, z_hi).
Axes of the slice: x: 4, y: 4, z: 8 (z_hi: 2, z_lo: 4; z = z_hi * 4 + z_lo), core: 2. Of those that a mesh axis runs over, the one named last changes fastest.
Arguments:
- x_ctx: bfloat16 [32768, 3072], P('dp', 'tensor'), may hold values from -0.16113281 to 0.16113281
- d_out: bfloat16 [32768, 3072], P(('dp', 'tensor')), may hold values from -2.390625 to 2.390625
- weight: bfloat16 [3072, 3072], P('tensor'), may hold values from -0.109375 to 0.109375
- error: bfloat16 [32, 3072, 3072], P('dp', 'tensor'), may hold values from -1.5 to 1.5
- q_init: float32 [32, 24576], P(None, 'tensor'), may hold values from -6 to 6
Outputs:
- d_input: bfloat16 [32768, 3072], P('dp', 'tensor')
- new_error: bfloat16 [32, 3072, 3072], P('dp', 'tensor')
- left_factor: float32 [32, 3072], P(None, 'tensor')
- right_factor: float32 [32, 24576], P(None, 'tensor')
The draws below stay inside these ranges and needn't reach their ends.
All inputs are finite; a program needn't handle non-finite values.
Results may differ from the reference program's by a relative error of at most 0.0006.
Values may be sent and summed in bfloat16 or wider, within the bound.
No kernel may reach another device: no remote copies, remote signals or barrier semaphores. Data moves between devices by JAX's collectives and lax.ppermute only.
A program may use at most 64 MiB of HBM per device.

```python
import jax
import jax.numpy as jnp
from jax import lax

DW = 3072
RANK = 32
ITERS = 3
TOK = 1024
DH = 3072
DHD = 384
TOKENS = 32768
QCOLS = 24576
N_DP = 32
N_TENSOR = 8


def steps_of(stream_key, shape, split, least, high):
    level = 1.0
    for axis_at, parts in split:
        draws = jax.random.uniform(jax.random.fold_in(jax.random.fold_in(stream_key, 6), axis_at), (parts,), jnp.float32, least / len(split), high / len(split))
        level = level * jnp.repeat(jnp.exp(draws), shape[axis_at] // parts).reshape((-1,) + (1,) * (len(shape) - 1 - axis_at))
    return level


def noise(rng, dims, width, limit, shards=(), dtype=jnp.bfloat16):
    result = jax.random.normal(rng, dims, jnp.float32) * width
    if len(shards) > 0:
        result = steps_of(rng, dims, shards, -0.22, 0.18) * result
    return jnp.clip(result, min=-limit, max=limit).astype(dtype)


def setup_inputs(seed: int = 0) -> dict:
    keys = jax.random.split(jax.random.key(seed), 6)
    x_ctx = noise(keys[0], (TOKENS, DH), 0.027, 0.16113281, ((0, 32), (1, 8)))
    d_out = noise(keys[1], (TOKENS, DW), 0.4, 2.390625, ((0, 256),))
    weight = noise(keys[2], (DH, DW), DW ** -0.5, 0.109375, ((0, 8),))
    error = noise(keys[3], (N_DP, DH, DW), 0.25, 1.5, ((0, 32), (1, 8)))
    q_init = noise(keys[4], (RANK, QCOLS), 1.0, 6.0, ((1, 8),), jnp.float32)
    return {"x_ctx": x_ctx, "d_out": d_out, "weight": weight, "error": error, "q_init": q_init}


PRECISE = lax.Precision.HIGHEST
EPSILON = 1e-06

def orthonormal_rows(matrix):
    row_count = matrix.shape[0]
    positions = jnp.arange(row_count)

    def one_row(row_index, current):
        vector_row = lax.dynamic_index_in_dim(current, row_index, 0, keepdims=False)
        projection = jnp.dot(current, vector_row, precision=PRECISE) * (positions < row_index)
        vector_row = vector_row - jnp.dot(projection, current, precision=PRECISE)
        vector_row = vector_row * lax.rsqrt(jnp.sum(vector_row * vector_row) + EPSILON)
        return lax.dynamic_update_index_in_dim(current, vector_row, row_index, 0)
    return lax.fori_loop(0, row_count, one_row, matrix)

def reference(x_ctx, d_out, weight, error, q_init):
    d_input = jnp.dot(d_out, weight.T, preferred_element_type=jnp.float32).astype(jnp.bfloat16)
    grads_all = d_out.astype(jnp.float32).reshape(N_DP, TOK, DW)
    context = x_ctx.reshape(N_DP, TOK, N_TENSOR, DHD).transpose(2, 0, 1, 3)
    errors = error.reshape(N_DP, N_TENSOR, DHD, DW).transpose(1, 0, 2, 3)
    starts = q_init.reshape(RANK, N_TENSOR, DW).transpose(1, 0, 2)

    def one_block(operands):
        context_block, error_block, right_rows = operands
        grad = jnp.einsum('rtk,rtc->rkc', context_block.astype(jnp.float32), grads_all, precision=PRECISE)
        merged = grad + error_block.astype(jnp.float32)
        left_rows = jnp.zeros((RANK, DHD), jnp.float32)
        for iteration in range(ITERS):
            left_rows = jnp.einsum('jc,rkc->jk', right_rows, merged, precision=PRECISE)
            left_rows = orthonormal_rows(left_rows)
            right_rows = jnp.einsum('jk,rkc->jc', left_rows, merged, precision=PRECISE) / N_DP
        approx = jnp.einsum('jk,jc->kc', left_rows, right_rows, precision=PRECISE)
        return (left_rows, right_rows, (merged - approx[None]).astype(jnp.bfloat16))
    lefts, rights, updated = lax.map(one_block, (context, errors, starts))
    left_factor = lefts.transpose(1, 0, 2).reshape(RANK, N_TENSOR * DHD)
    right_factor = rights.transpose(1, 0, 2).reshape(RANK, N_TENSOR * DW)
    new_error = updated.transpose(1, 0, 2, 3).reshape(N_DP, N_TENSOR * DHD, DW)
    return (d_input, new_error, left_factor, right_factor)
```

```python
import functools

import jax
import jax.numpy as jnp
import numpy as np
from jax import lax
from jax.experimental import pallas as pl
from jax.experimental.pallas import tpu as pltpu
from jax.sharding import Mesh, PartitionSpec as P

ITERS = 3
CHUNKS = 3
EPSILON = 1e-06
PRECISE = lax.Precision.HIGHEST
DP = ("y", "zl", "c")
TENSOR = ("x", "zh")
SIZES = {"y": 4, "zl": 4, "c": 2, "x": 4, "zh": 2}
CONTRACT_LAST = (((1,), (1,)), ((), ()))
CONTRACT_FIRST = (((0,), (0,)), ((), ()))


def shift(value, axis, by):
    n = SIZES[axis]
    return lax.ppermute(value, axis, [(i, (i + by) % n) for i in range(n)])


def swap(value, axis, by):
    return lax.ppermute(value, axis, [(i, i ^ by) for i in range(SIZES[axis])])


def gather_tokens(block):
    rows, width = block.shape
    x, zh = lax.axis_index("x"), lax.axis_index("zh")
    own_before, own_after = shift(block, "x", 1), shift(block, "x", -1)
    other = swap(block, "zh", 1)
    own_far = shift(own_after, "x", -1)
    other_before, other_after = shift(other, "x", 1), shift(other, "x", -1)
    other_far = shift(other_before, "x", 1)
    whole = jnp.zeros((rows * 8, width), block.dtype)
    for by, own, oth in (
        (0, block, other),
        (3, own_before, other_before),
        (1, own_after, other_after),
        (2, own_far, other_far),
    ):
        at = ((x + by) % 4) * 2
        whole = lax.dynamic_update_slice(whole, own, ((at + zh) * rows, 0))
        whole = lax.dynamic_update_slice(whole, oth, ((at + 1 - zh) * rows, 0))
    return whole


def sum_half(merged):
    features, width = merged.shape
    y, zl, c = lax.axis_index("y"), lax.axis_index("zl"), lax.axis_index("c")
    half = width // 2
    sent = swap(lax.dynamic_slice(merged, (0, (1 - c) * half), (features, half)), "c", 1)
    total = lax.dynamic_slice(merged, (0, c * half), (features, half)) + sent
    quarter = features // 4

    def piece(at):
        return lax.dynamic_slice(total, (at % 4 * quarter, 0), (quarter, half))

    part = piece(y)
    for by in (1, 2, 3):
        part = part + shift(piece(y + by), "y", by)
    small = quarter // 4

    def subpiece(at):
        return lax.dynamic_slice(part, (at * small, 0), (small, half))

    last = subpiece(zl)
    for by in (1, 2, 3):
        last = last + swap(subpiece(zl ^ by), "zl", by)
    out = jnp.zeros((quarter, half), merged.dtype)
    out = lax.dynamic_update_slice(out, last, (zl * small, 0))
    for by in (1, 2, 3):
        out = lax.dynamic_update_slice(out, swap(last, "zl", by), ((zl ^ by) * small, 0))
    whole = jnp.zeros((features, half), merged.dtype)
    whole = lax.dynamic_update_slice(whole, out, (y * quarter, 0))
    for by in (1, 2, 3):
        whole = lax.dynamic_update_slice(whole, shift(out, "y", by), ((y - by) % 4 * quarter, 0))
    return whole


def orthonormal(matrix):
    taken = jnp.zeros_like(matrix)
    rows = []
    for j in range(matrix.shape[0]):
        row = matrix[j : j + 1, :] - taken[j : j + 1, :]
        scale = lax.rsqrt(jnp.sum(row * row, axis=1, keepdims=True) + EPSILON)
        along = jnp.sum(matrix * row, axis=1, keepdims=True) * scale
        row = row * scale
        rows.append(row)
        taken = taken + along * row
    return jnp.concatenate(rows, axis=0)


def iterate_kernel(replicas, left_ref, gram_ref, out_ref):
    left = orthonormal(left_ref[...])
    for _ in range(ITERS - 1):
        left = jnp.dot(left, gram_ref[...], precision=PRECISE, preferred_element_type=jnp.float32)
        left = orthonormal(left * (1.0 / replicas))
    out_ref[...] = left


def iterate(left, gram, replicas):
    return pl.pallas_call(
        functools.partial(iterate_kernel, replicas),
        out_shape=jax.ShapeDtypeStruct(left.shape, jnp.float32),
        in_specs=[pl.BlockSpec(memory_space=pltpu.VMEM)] * 2,
        out_specs=pl.BlockSpec(memory_space=pltpu.VMEM),
        name="iterate",
    )(left, gram)


def on_device(x_ctx, d_out, weight, error, q_init):
    replicas = 32
    c = lax.axis_index("c")
    columns = d_out.shape[1]
    width = columns // CHUNKS
    half = width // 2
    merged, halves = [], []
    d_input = 0.0
    products = 0.0
    for i in range(CHUNKS):
        cols = slice(i * width, (i + 1) * width)
        tokens = gather_tokens(d_out[:, cols])
        grad = lax.dot_general(x_ctx, tokens, CONTRACT_FIRST, preferred_element_type=jnp.float32)
        merged.append(grad + error[0, :, cols].astype(jnp.float32))
        d_input = d_input + lax.dot_general(
            tokens, weight[:, cols], CONTRACT_LAST, preferred_element_type=jnp.float32
        )
        mine = sum_half(merged[-1])
        halves.append(mine)
        start = lax.dynamic_slice(q_init, (0, i * width + c * half), (q_init.shape[0], half))
        rows = jnp.concatenate([start, mine], axis=0)
        products = products + lax.dot_general(rows, mine, CONTRACT_LAST, precision=PRECISE)
    products = products + swap(products, "c", 1)
    rank = q_init.shape[0]
    left = iterate(products[:rank], products[rank:], replicas)
    mine = jnp.dot(left, jnp.concatenate(halves, axis=1), precision=PRECISE) / replicas
    other = swap(mine, "c", 1)
    mine, other = mine.reshape(rank, CHUNKS, 1, half), other.reshape(rank, CHUNKS, 1, half)
    first = jnp.where(c == 0, mine, other)
    second = jnp.where(c == 0, other, mine)
    right = jnp.concatenate([first, second], axis=2).reshape(rank, columns)
    approx = lax.dot_general(left, right, CONTRACT_FIRST, precision=PRECISE)
    new_error = (jnp.concatenate(merged, axis=1) - approx).astype(jnp.bfloat16)[None]
    return d_input.astype(jnp.bfloat16), new_error, left, right


def solution(mesh):
    names = ("y", "zl", "c", "x", "zh")
    fine = Mesh(mesh.devices.reshape([SIZES[name] for name in names]), names)
    return jax.shard_map(
        on_device,
        mesh=fine,
        in_specs=(
            P(DP, TENSOR),
            P(DP + TENSOR, None),
            P(TENSOR, None),
            P(DP, TENSOR, None),
            P(None, TENSOR),
        ),
        out_specs=(
            P(DP, TENSOR),
            P(DP, TENSOR, None),
            P(None, TENSOR),
            P(None, TENSOR),
        ),
        check_vma=False,
    )
```

```python
import functools
import math

import jax
import jax.numpy as jnp
from jax import lax
from jax.experimental import pallas as pl
from jax.experimental.pallas import tpu as pltpu
from jax.sharding import Mesh, PartitionSpec as P

ITERS = 3
EPSILON = 1e-06
DP = ("y", "zl", "c")
TENSOR = ("x", "zh")
SIZES = {"y": 4, "zl": 4, "c": 2, "x": 4, "zh": 2}
THIRDS = ((0, 2), (2, 1))
CONTRACT_LAST = (((1,), (1,)), ((), ()))
CONTRACT_FIRST = (((0,), (0,)), ((), ()))
LIMIT = 48 * 1024 * 1024
F32, BF16 = jnp.float32, jnp.bfloat16
STEP = 16

RATIO = 512.0
POWER = 250.0 / math.log2(RATIO + math.sqrt(RATIO * RATIO + 1.0))


def encode(value, scale):
    t = jnp.abs(value) * (RATIO / scale)
    code = jnp.exp2(POWER * jnp.log2(t + jnp.sqrt(t * t + 1.0)) - 125.0)
    return jnp.where(value < 0, -code, code).astype(BF16)


def decode(code, scale):
    code = code.astype(F32)
    t = jnp.exp2((jnp.log2(jnp.abs(code)) + 125.0) * (1.0 / POWER))
    value = (t - 1.0 / t) * (scale * (0.5 / RATIO))
    return jnp.where(code < 0, -value, value)


def split(value):
    high = value.astype(BF16)
    return high, (value - high.astype(F32)).astype(BF16)


def shift(value, axis, by):
    n = SIZES[axis]
    return lax.ppermute(value, axis, [(i, (i + by) % n) for i in range(n)])


def swap(value, axis, by):
    return lax.ppermute(value, axis, [(i, i ^ by) for i in range(SIZES[axis])])


def whole(*arrays):
    return [pl.BlockSpec(memory_space=pltpu.VMEM) for _ in arrays]


def call(kernel, name, place, arrays, outs, scratch=(), flops=0):
    nbytes = sum(a.size * a.dtype.itemsize for a in (*arrays, *outs))
    return pl.pallas_call(
        kernel,
        out_shape=tuple(outs),
        in_specs=[pl.BlockSpec(memory_space=pltpu.SMEM)] + whole(*arrays),
        out_specs=tuple(whole(*outs)),
        scratch_shapes=list(scratch),
        compiler_params=pltpu.CompilerParams(vmem_limit_bytes=LIMIT),
        cost_estimate=pl.CostEstimate(flops=flops, bytes_accessed=nbytes, transcendentals=0),
        name=name,
    )(place, *arrays)


def shape(dims, dtype):
    return jax.ShapeDtypeStruct(dims, dtype)


def steps(rows, body):
    @pl.loop(0, rows // STEP)
    def _(i):
        body(pl.ds(pl.multiple_of(i * STEP, STEP), STEP), i)


def rows_at(start, i):
    return pl.ds(pl.multiple_of(start + i * STEP, STEP), STEP)


def block_order(place_ref):
    x, zh = place_ref[3], place_ref[4]
    order = []
    for by in (0, 3, 1, 2):
        at = lax.rem(x + by, 4) * 2
        order += [at + zh, at + 1 - zh]
    return order


def merge_kernel(place_ref, xt_ref, error_ref, *refs):
    blocks, (merged_ref, send_ref, x_ref) = refs[:8], refs[8:]
    rows, width = blocks[0].shape
    for b, at in enumerate(block_order(place_ref)):
        x_ref[:, b * rows : (b + 1) * rows] = xt_ref[:, pl.ds(pl.multiple_of(at * rows, rows), rows)]
    tile = min(width, 512)
    for k in range(width // tile):
        cols = slice(k * tile, (k + 1) * tile)
        tokens = jnp.concatenate([ref[:, cols] for ref in blocks], axis=0)
        grad = jnp.dot(x_ref[...], tokens, preferred_element_type=F32)
        merged_ref[:, cols] = grad + error_ref[:, cols].astype(F32)
    half = width // 2
    there = pl.multiple_of((1 - place_ref[2]) * half, half)

    def body(rows, _):
        send_ref[rows, :] = merged_ref[rows, pl.ds(there, half)]

    steps(merged_ref.shape[0], body)


def pack_y_kernel(place_ref, merged_ref, got_ref, own_ref, p1_ref, p2_ref, p3_ref, scale_ref, total_ref, top_ref):
    y, c = place_ref[0], place_ref[2]
    features, half = got_ref.shape
    quarter = features // 4
    here = pl.multiple_of(c * half, half)
    top_ref[...] = jnp.zeros_like(top_ref)

    def add(rows, _):
        total = merged_ref[rows, pl.ds(here, half)] + got_ref[rows, :]
        total_ref[rows, :] = total
        top_ref[...] = jnp.maximum(top_ref[...], jnp.abs(total))

    steps(features, add)
    top = jnp.max(jnp.max(top_ref[...], axis=0, keepdims=True), axis=1, keepdims=True)
    scale = jnp.maximum(top * 1.004, 1e-30).astype(BF16).astype(F32)
    scale_ref[...] = jnp.broadcast_to(scale, scale_ref.shape)
    starts = [lax.rem(y + k, 4) * quarter for k in range(4)]

    def pack(rows, i):
        own_ref[rows, :] = total_ref[rows_at(starts[0], i), :]
        for k, ref in ((1, p1_ref), (2, p2_ref), (3, p3_ref)):
            ref[rows, :] = encode(total_ref[rows_at(starts[k], i), :], scale)

    steps(quarter, pack)
    for ref in (p1_ref, p2_ref, p3_ref):
        ref[quarter:, :] = jnp.broadcast_to(scale, (STEP, half)).astype(BF16)


def scale_of(ref, rows):
    return ref[rows:, :][0:1, 0:1].astype(F32)


def turn_kernel(place_ref, own_ref, scale_ref, r1_ref, r2_ref, r3_ref, mine_ref, q1_ref, q2_ref, q3_ref, next_ref, part_ref):
    zl = place_ref[1]
    quarter, half = own_ref.shape
    small = half // 4
    got = (r1_ref, r2_ref, r3_ref)
    scales = [scale_of(ref, quarter) for ref in got]
    scale = scale_ref[0:1, 0:1]
    for other in scales:
        scale = jnp.maximum(scale, other)
    scale = scale * 4.0
    next_ref[...] = jnp.broadcast_to(scale, next_ref.shape)

    def body(rows, _):
        part = own_ref[rows, :]
        for ref, other in zip(got, scales):
            part = part + decode(ref[rows, :], other)
        part_ref[rows, :] = part

    steps(quarter, body)

    def piece(rows, k):
        at = lax.bitwise_xor(zl, k) * small
        return part_ref[rows, pl.ds(pl.multiple_of(at, small), small)]

    def pack(rows, _):
        mine_ref[rows, :] = piece(rows, 0)
        for k, ref in ((1, q1_ref), (2, q2_ref), (3, q3_ref)):
            ref[rows, :] = encode(piece(rows, k), scale)

    steps(quarter, pack)
    for ref in (q1_ref, q2_ref, q3_ref):
        ref[quarter:, :] = jnp.broadcast_to(scale, (STEP, small)).astype(BF16)


def finish_kernel(place_ref, mine_ref, scale_ref, r1_ref, r2_ref, r3_ref, code_ref, last_ref):
    quarter, _ = mine_ref.shape
    got = (r1_ref, r2_ref, r3_ref)
    scales = [scale_of(ref, quarter) for ref in got]
    scale = scale_ref[0:1, 0:1]
    for other in scales:
        scale = jnp.maximum(scale, other)
    scale = scale * 4.0
    last_ref[...] = jnp.broadcast_to(scale, last_ref.shape)

    def body(rows, _):
        total = mine_ref[rows, :]
        for ref, other in zip(got, scales):
            total = total + decode(ref[rows, :], other)
        code_ref[rows, :] = encode(total, scale)

    steps(quarter, body)


def unpack(place_ref, own_ref, other_ref, own_scale_ref, other_scale_ref, high_ref, low_ref, base):
    c = place_ref[2]
    features, half = own_ref.shape
    own_scale, other_scale = own_scale_ref[0:1, 0:1], other_scale_ref[0:1, 0:1]

    def body(rows, _):
        for ref, scale, at in ((own_ref, own_scale, c), (other_ref, other_scale, 1 - c)):
            high, low = split(decode(ref[rows, :], scale))
            cols = pl.ds(pl.multiple_of(base + at * half, half), half)
            high_ref[rows, cols] = high
            low_ref[rows, cols] = low

    steps(features, body)


def gram(start, high, low):
    start_high, start_low = split(start)
    rows_high = jnp.concatenate([start_high, high], axis=0)
    rows_low = jnp.concatenate([start_low, low], axis=0)
    total = lax.dot_general(rows_high, high, CONTRACT_LAST, preferred_element_type=F32)
    total = total + lax.dot_general(rows_high, low, CONTRACT_LAST, preferred_element_type=F32)
    return total + lax.dot_general(rows_low, high, CONTRACT_LAST, preferred_element_type=F32)


def first_kernel(place_ref, own_ref, other_ref, own_scale_ref, other_scale_ref, start_ref, high_ref, low_ref, gram_ref):
    unpack(place_ref, own_ref, other_ref, own_scale_ref, other_scale_ref, high_ref, low_ref, 0)
    gram_ref[...] = gram(start_ref[...], high_ref[...], low_ref[...])


def orthonormal(matrix):
    taken = jnp.zeros_like(matrix)
    rows = []
    for j in range(matrix.shape[0]):
        row = matrix[j : j + 1, :] - taken[j : j + 1, :]
        scale = lax.rsqrt(jnp.sum(row * row, axis=1, keepdims=True) + EPSILON)
        along = jnp.sum(matrix * row, axis=1, keepdims=True) * scale
        row = row * scale
        rows.append(row)
        taken = taken + along * row
    return jnp.concatenate(rows, axis=0)


def times(left, high, low):
    rank = left.shape[0]
    left_high, left_low = split(left)
    both = jnp.dot(jnp.concatenate([left_high, left_low], axis=0), high, preferred_element_type=F32)
    return both[:rank] + both[rank:] + jnp.dot(left_high, low, preferred_element_type=F32)


def last_kernel(
    replicas, place_ref, own_ref, other_ref, own_scale_ref, other_scale_ref, start_ref, first_high_ref, first_low_ref,
    first_gram_ref, merged_a_ref, merged_b_ref, error_ref, left_ref, right_ref, high_ref, low_ref,
):
    rank = start_ref.shape[0]
    unpack(place_ref, own_ref, other_ref, own_scale_ref, other_scale_ref, high_ref, low_ref, 0)
    products = first_gram_ref[...] + gram(start_ref[...], high_ref[...], low_ref[...])
    left = orthonormal(products[:rank])
    gram_high, gram_low = split(products[rank:])
    for _ in range(ITERS - 1):
        left = orthonormal(times(left, gram_high, gram_low) * (1.0 / replicas))
    left_ref[...] = left
    left_high, left_low = split(left)
    left_parts = jnp.concatenate([left_high, left_high, left_low], axis=0)
    base = 0
    for hi_ref, lo_ref, merged_ref in (
        (first_high_ref, first_low_ref, merged_a_ref),
        (high_ref, low_ref, merged_b_ref),
    ):
        width = merged_ref.shape[1]
        tile = min(width, 512)
        for k in range(width // tile):
            cols = slice(k * tile, (k + 1) * tile)
            out = slice(base + k * tile, base + (k + 1) * tile)
            right = times(left, hi_ref[:, cols], lo_ref[:, cols]) * (1.0 / replicas)
            right_ref[:, out] = right
            right_high, right_low = split(right)
            right_parts = jnp.concatenate([right_high, right_low, right_high], axis=0)
            approx = lax.dot_general(left_parts, right_parts, CONTRACT_FIRST, preferred_element_type=F32)
            error_ref[:, out] = (merged_ref[:, cols] - approx).astype(BF16)
        base += width


def input_kernel(place_ref, weight_ref, *refs):
    blocks, (out_ref, acc_ref) = refs[:16], refs[16:]
    rows = blocks[0].shape[0]
    base = 0
    for chunk in (blocks[:8], blocks[8:]):
        width = chunk[0].shape[1]
        tile = min(width, 512)
        for k in range(width // tile):
            cols = slice(k * tile, (k + 1) * tile)
            tokens = jnp.concatenate([ref[:, cols] for ref in chunk], axis=0)
            w = weight_ref[:, base + k * tile : base + (k + 1) * tile]
            value = lax.dot_general(tokens, w, CONTRACT_LAST, preferred_element_type=F32)
            if base + k == 0:
                acc_ref[...] = value
            else:
                acc_ref[...] += value
        base += width
    for b, at in enumerate(block_order(place_ref)):
        out_ref[pl.ds(pl.multiple_of(at * rows, rows), rows), :] = acc_ref[b * rows : (b + 1) * rows, :].astype(BF16)


def gather_tokens(block):
    own_before, own_after = shift(block, "x", 1), shift(block, "x", -1)
    other = swap(block, "zh", 1)
    own_far = shift(own_after, "x", -1)
    other_before, other_after = shift(other, "x", 1), shift(other, "x", -1)
    other_far = shift(other_before, "x", 1)
    return [block, other, own_before, other_before, own_after, other_after, own_far, other_far]


def choose(index, options):
    value = options[3]
    for k in (2, 1, 0):
        value = jnp.where(index == k, options[k], value)
    return value


def sum_over_replicas(place, merged, send):
    features, half = send.shape
    quarter, small = features // 4, half // 4
    y, zl = place[0], place[1]
    got = swap(send, "c", 1)
    packet = shape((quarter + STEP, half), BF16)
    tag = shape((8, 128), F32)
    own, p1, p2, p3, scale = call(
        pack_y_kernel, "pack_y", place, (merged, got),
        (shape((quarter, half), F32), packet, packet, packet, tag),
        (pltpu.VMEM((features, half), F32), pltpu.VMEM((STEP, half), F32)),
    )
    r1, r2, r3 = (shift(p, "y", k) for k, p in ((1, p1), (2, p2), (3, p3)))
    packet = shape((quarter + STEP, small), BF16)
    mine, q1, q2, q3, scale = call(
        turn_kernel, "turn", place, (own, scale, r1, r2, r3),
        (shape((quarter, small), F32), packet, packet, packet, tag),
        (pltpu.VMEM((quarter, half), F32),),
    )
    r1, r2, r3 = (swap(q, "zl", k) for k, q in ((1, q1), (2, q2), (3, q3)))
    code, scale = call(
        finish_kernel, "finish", place, (mine, scale, r1, r2, r3), (shape((quarter, small), BF16), tag)
    )
    other_scale = swap(scale, "c", 1)
    pieces = [code] + [swap(code, "zl", k) for k in (1, 2, 3)]
    line = jnp.concatenate([choose(zl, [pieces[j ^ k] for k in range(4)]) for j in range(4)], axis=1)
    lines = [line] + [shift(line, "y", k) for k in (1, 2, 3)]
    mine = jnp.concatenate([choose(y, [lines[(k - j) % 4] for k in range(4)]) for j in range(4)], axis=0)
    return mine, swap(mine, "c", 1), scale, other_scale


def on_device(replicas, x_ctx, d_out, weight, error, q_init):
    place = jnp.stack([lax.axis_index(name) for name in ("y", "zl", "c", "x", "zh")]).astype(jnp.int32)
    columns = d_out.shape[1]
    features = x_ctx.shape[1]
    rank = q_init.shape[0]
    third = columns // 3
    xt = x_ctx.T
    chunks = [slice(a * third, (a + n) * third) for a, n in THIRDS]
    tokens = [gather_tokens(d_out[:, cols]) for cols in chunks]
    merged, sums = [], []
    for cols, blocks in zip(chunks, tokens):
        width = cols.stop - cols.start
        whole_chunk, send = call(
            merge_kernel, "merge", place, (xt, error[0, :, cols], *blocks),
            (shape((features, width), F32), shape((features, width // 2), F32)),
            (pltpu.VMEM(xt.shape, BF16),), 2 * xt.size * width,
        )
        merged.append(whole_chunk)
        sums.append(sum_over_replicas(place, whole_chunk, send))
    (d_input,) = call(
        input_kernel, "d_input", place, (weight, *tokens[0], *tokens[1]), (shape(x_ctx.shape, BF16),),
        (pltpu.VMEM(x_ctx.shape, F32),), 2 * x_ctx.size * columns,
    )
    wide = shape((features, 2 * third), BF16)
    high, low, products = call(
        first_kernel, "first", place, (*sums[0], q_init[:, chunks[0]]),
        (wide, wide, shape((rank + features, features), F32)),
    )
    wide = pltpu.VMEM((features, third), BF16)
    new_error, left, right = call(
        functools.partial(last_kernel, replicas), "last", place,
        (*sums[1], q_init[:, chunks[1]], high, low, products, *merged),
        (shape((features, columns), BF16), shape((rank, features), F32), shape((rank, columns), F32)),
        (wide, wide),
    )
    return d_input, new_error[None], left, right


def solution(mesh):
    names = ("y", "zl", "c", "x", "zh")
    fine = Mesh(mesh.devices.reshape([SIZES[name] for name in names]), names)
    return jax.shard_map(
        functools.partial(on_device, mesh.shape["dp"]),
        mesh=fine,
        in_specs=(
            P(DP, TENSOR),
            P(DP + TENSOR, None),
            P(TENSOR, None),
            P(DP, TENSOR, None),
            P(None, TENSOR),
        ),
        out_specs=(
            P(DP, TENSOR),
            P(DP, TENSOR, None),
            P(None, TENSOR),
            P(None, TENSOR),
        ),
        check_vma=False,
    )
```

```python
import functools
import math

import jax
import jax.numpy as jnp
from jax import lax
from jax.experimental import pallas as pl
from jax.experimental.pallas import tpu as pltpu
from jax.sharding import Mesh, PartitionSpec as P

ITERS = 3
EPSILON = 1e-06
DP = ("y", "zl", "c")
TENSOR = ("x", "zh")
SIZES = {"y": 4, "zl": 4, "c": 2, "x": 4, "zh": 2}
THIRDS = ((0, 2), (2, 1))
CONTRACT_LAST = (((1,), (1,)), ((), ()))
CONTRACT_FIRST = (((0,), (0,)), ((), ()))
LIMIT = 20 * 1024 * 1024
F32, BF16 = jnp.float32, jnp.bfloat16
STEP = 16

RATIO = 512.0
POWER = 250.0 / math.log2(RATIO + math.sqrt(RATIO * RATIO + 1.0))


def encode(value, scale):
    t = jnp.abs(value) * (RATIO / scale)
    code = jnp.exp2(POWER * jnp.log2(t + jnp.sqrt(t * t + 1.0)) - 125.0)
    return jnp.where(value < 0, -code, code).astype(BF16)


def decode(code, scale):
    code = code.astype(F32)
    t = jnp.exp2((jnp.log2(jnp.abs(code)) + 125.0) * (1.0 / POWER))
    value = (t - 1.0 / t) * (scale * (0.5 / RATIO))
    return jnp.where(code < 0, -value, value)


def split(value):
    high = value.astype(BF16)
    return high, (value - high.astype(F32)).astype(BF16)


def shift(value, axis, by):
    n = SIZES[axis]
    return lax.ppermute(value, axis, [(i, (i + by) % n) for i in range(n)])


def swap(value, axis, by):
    return lax.ppermute(value, axis, [(i, i ^ by) for i in range(SIZES[axis])])


def whole(*arrays):
    return [pl.BlockSpec(memory_space=pltpu.VMEM) for _ in arrays]


def call(kernel, name, place, arrays, outs, scratch=(), flops=0, after=()):

    def body(place_ref, *refs):
        kernel(place_ref, *refs[len(after) :])

    return pl.pallas_call(
        body,
        out_shape=tuple(outs),
        in_specs=[pl.BlockSpec(memory_space=pltpu.SMEM)]
        + [pl.BlockSpec(memory_space=pl.ANY)] * len(after)
        + whole(*arrays),
        out_specs=tuple(whole(*outs)),
        scratch_shapes=list(scratch),
        compiler_params=pltpu.CompilerParams(vmem_limit_bytes=LIMIT),
        cost_estimate=pl.CostEstimate(flops=0, bytes_accessed=0, transcendentals=0),
        name=name,
    )(place, *after, *arrays)


def shape(dims, dtype):
    return jax.ShapeDtypeStruct(dims, dtype)


def steps(rows, body):
    @pl.loop(0, rows // STEP)
    def _(i):
        body(pl.ds(pl.multiple_of(i * STEP, STEP), STEP), i)


def rows_at(start, i):
    return pl.ds(pl.multiple_of(start + i * STEP, STEP), STEP)


def block_order(place_ref):
    x, zh = place_ref[3], place_ref[4]
    order = []
    for by in (0, 3, 1, 2):
        at = lax.rem(x + by, 4) * 2
        order += [at + zh, at + 1 - zh]
    return order


def merge_kernel(base, place_ref, xt_ref, error_ref, *refs):
    blocks, (merged_ref, send_ref, tag_ref, x_ref, top_ref) = refs[:8], refs[8:]
    rows, width = blocks[0].shape
    features = merged_ref.shape[0]
    for b, at in enumerate(block_order(place_ref)):
        x_ref[:, b * rows : (b + 1) * rows] = xt_ref[:, pl.ds(pl.multiple_of(at * rows, rows), rows)]
    tile = min(width, 512)
    for k in range(width // tile):
        cols = slice(k * tile, (k + 1) * tile)
        tokens = jnp.concatenate([ref[:, cols] for ref in blocks], axis=0)
        grad = jnp.dot(x_ref[...], tokens, preferred_element_type=F32)
        merged_ref[:, cols] = grad + error_ref[:, base + k * tile : base + (k + 1) * tile].astype(F32)
    half = width // 2
    here = pl.multiple_of(place_ref[2] * half, half)
    there = pl.multiple_of((1 - place_ref[2]) * half, half)
    top_ref[...] = jnp.zeros_like(top_ref)

    def body(rows, _):
        sent = merged_ref[rows, pl.ds(there, half)]
        send_ref[rows, :] = sent
        kept = merged_ref[rows, pl.ds(here, half)]
        top_ref[...] = jnp.maximum(top_ref[...], jnp.maximum(jnp.abs(sent), jnp.abs(kept)))

    steps(features, body)
    top = jnp.max(jnp.max(top_ref[...], axis=0, keepdims=True), axis=1, keepdims=True)
    send_ref[features:, :] = jnp.broadcast_to(top, (8, half))
    tag_ref[...] = jnp.broadcast_to(top, tag_ref.shape)


def pack_y_kernel(place_ref, merged_ref, tag_ref, got_ref, own_ref, p1_ref, p2_ref, p3_ref, scale_ref):
    y, c = place_ref[0], place_ref[2]
    quarter, half = own_ref.shape
    features = 4 * quarter
    here = pl.multiple_of(c * half, half)
    top = jnp.maximum(tag_ref[0:1, 0:1], got_ref[features:, :][0:1, 0:1])
    scale = jnp.maximum(top * 2.008, 1e-30).astype(BF16).astype(F32)
    scale_ref[...] = jnp.broadcast_to(scale, scale_ref.shape)
    starts = [lax.rem(y + k, 4) * quarter for k in range(4)]

    def total(start, i):
        rows = rows_at(start, i)
        return merged_ref[rows, pl.ds(here, half)] + got_ref[rows, :]

    def pack(rows, i):
        own_ref[rows, :] = total(starts[0], i)
        for k, ref in ((1, p1_ref), (2, p2_ref), (3, p3_ref)):
            ref[rows, :] = encode(total(starts[k], i), scale)

    steps(quarter, pack)
    for ref in (p1_ref, p2_ref, p3_ref):
        ref[quarter:, :] = jnp.broadcast_to(scale, (STEP, half)).astype(BF16)


def scale_of(ref, rows):
    return ref[rows:, :][0:1, 0:1].astype(F32)


def turn_kernel(place_ref, own_ref, scale_ref, r1_ref, r2_ref, r3_ref, mine_ref, q1_ref, q2_ref, q3_ref, next_ref, part_ref):
    zl = place_ref[1]
    quarter, half = own_ref.shape
    small = half // 4
    got = (r1_ref, r2_ref, r3_ref)
    scales = [scale_of(ref, quarter) for ref in got]
    scale = scale_ref[0:1, 0:1]
    for other in scales:
        scale = jnp.maximum(scale, other)
    scale = scale * 4.0
    next_ref[...] = jnp.broadcast_to(scale, next_ref.shape)

    def body(rows, _):
        part = own_ref[rows, :]
        for ref, other in zip(got, scales):
            part = part + decode(ref[rows, :], other)
        part_ref[rows, :] = part

    steps(quarter, body)

    def piece(rows, k):
        at = lax.bitwise_xor(zl, k) * small
        return part_ref[rows, pl.ds(pl.multiple_of(at, small), small)]

    def pack(rows, _):
        mine_ref[rows, :] = piece(rows, 0)
        for k, ref in ((1, q1_ref), (2, q2_ref), (3, q3_ref)):
            ref[rows, :] = encode(piece(rows, k), scale)

    steps(quarter, pack)
    for ref in (q1_ref, q2_ref, q3_ref):
        ref[quarter:, :] = jnp.broadcast_to(scale, (STEP, small)).astype(BF16)


def finish_kernel(place_ref, mine_ref, scale_ref, r1_ref, r2_ref, r3_ref, code_ref, last_ref):
    quarter, _ = mine_ref.shape
    got = (r1_ref, r2_ref, r3_ref)
    scales = [scale_of(ref, quarter) for ref in got]
    scale = scale_ref[0:1, 0:1]
    for other in scales:
        scale = jnp.maximum(scale, other)
    scale = scale * 4.0
    last_ref[...] = jnp.broadcast_to(scale, last_ref.shape)

    def body(rows, _):
        total = mine_ref[rows, :]
        for ref, other in zip(got, scales):
            total = total + decode(ref[rows, :], other)
        code_ref[rows, :] = encode(total, scale)

    steps(quarter, body)


def unpack(place_ref, own_ref, other_ref, scale_ref, high_ref, low_ref):
    c = place_ref[2]
    features, half = own_ref.shape
    scale = scale_ref[0:1, 0:1]

    def body(rows, _):
        for ref, at in ((own_ref, c), (other_ref, 1 - c)):
            high, low = split(decode(ref[rows, :], scale))
            cols = pl.ds(pl.multiple_of(at * half, half), half)
            high_ref[rows, cols] = high
            low_ref[rows, cols] = low

    steps(features, body)


def gram(start, high, low):
    start_high, start_low = split(start)
    rows_high = jnp.concatenate([start_high, high], axis=0)
    rows_low = jnp.concatenate([start_low, low], axis=0)
    total = lax.dot_general(rows_high, high, CONTRACT_LAST, preferred_element_type=F32)
    total = total + lax.dot_general(rows_high, low, CONTRACT_LAST, preferred_element_type=F32)
    return total + lax.dot_general(rows_low, high, CONTRACT_LAST, preferred_element_type=F32)


def first_kernel(base, place_ref, own_ref, other_ref, scale_ref, start_ref, *refs):
    *before, high_ref, low_ref, gram_ref = refs
    unpack(place_ref, own_ref, other_ref, scale_ref, high_ref, low_ref)
    width = high_ref.shape[1]
    products = gram(start_ref[:, base : base + width], high_ref[...], low_ref[...])
    for ref in before:
        products = products + ref[...]
    gram_ref[...] = products


def orthonormal(matrix):
    taken = jnp.zeros_like(matrix)
    rows = []
    for j in range(matrix.shape[0]):
        row = matrix[j : j + 1, :] - taken[j : j + 1, :]
        scale = lax.rsqrt(jnp.sum(row * row, axis=1, keepdims=True) + EPSILON)
        along = jnp.sum(matrix * row, axis=1, keepdims=True) * scale
        row = row * scale
        rows.append(row)
        taken = taken + along * row
    return jnp.concatenate(rows, axis=0)


def times(left, high, low):
    rank = left.shape[0]
    left_high, left_low = split(left)
    both = jnp.dot(jnp.concatenate([left_high, left_low], axis=0), high, preferred_element_type=F32)
    return both[:rank] + both[rank:] + jnp.dot(left_high, low, preferred_element_type=F32)


def last_kernel(replicas, place_ref, own_ref, other_ref, scale_ref, start_ref, products_ref, *refs):
    *earlier, merged_ref, left_ref, right_ref, error_ref, high_ref, low_ref = refs
    parts = [tuple(earlier[i : i + 3]) for i in range(0, len(earlier), 3)] + [(high_ref, low_ref, merged_ref)]
    rank, columns = right_ref.shape
    width = merged_ref.shape[1]
    unpack(place_ref, own_ref, other_ref, scale_ref, high_ref, low_ref)
    products = products_ref[...] + gram(start_ref[:, columns - width :], high_ref[...], low_ref[...])
    left = orthonormal(products[:rank])
    gram_high, gram_low = split(products[rank:])
    for _ in range(ITERS - 1):
        left = orthonormal(times(left, gram_high, gram_low) * (1.0 / replicas))
    left_ref[...] = left
    left_high, left_low = split(left)
    left_parts = jnp.concatenate([left_high, left_high, left_low], axis=0)
    base = 0
    for hi_ref, lo_ref, merged in parts:
        width = merged.shape[1]
        tile = min(width, 512)
        for k in range(width // tile):
            cols = slice(k * tile, (k + 1) * tile)
            out = slice(base + k * tile, base + (k + 1) * tile)
            right = times(left, hi_ref[:, cols], lo_ref[:, cols]) * (1.0 / replicas)
            right_ref[:, out] = right
            right_high, right_low = split(right)
            right_parts = jnp.concatenate([right_high, right_low, right_high], axis=0)
            approx = lax.dot_general(left_parts, right_parts, CONTRACT_FIRST, preferred_element_type=F32)
            error_ref[:, out] = (merged[:, cols] - approx).astype(BF16)
        base += width


def input_kernel(place_ref, weight_ref, *refs):
    *blocks, out_ref, acc_ref = refs
    rows = blocks[0].shape[0]
    base = 0
    for chunk in [blocks[i : i + 8] for i in range(0, len(blocks), 8)]:
        width = chunk[0].shape[1]
        tile = min(width, 512)
        for k in range(width // tile):
            cols = slice(k * tile, (k + 1) * tile)
            tokens = jnp.concatenate([ref[:, cols] for ref in chunk], axis=0)
            w = weight_ref[:, base + k * tile : base + (k + 1) * tile]
            value = lax.dot_general(tokens, w, CONTRACT_LAST, preferred_element_type=F32)
            if base + k == 0:
                acc_ref[...] = value
            else:
                acc_ref[...] += value
        base += width
    for b, at in enumerate(block_order(place_ref)):
        out_ref[pl.ds(pl.multiple_of(at * rows, rows), rows), :] = acc_ref[b * rows : (b + 1) * rows, :].astype(BF16)


def gather_tokens(first, second):
    own, other = [], []
    for block, way in ((first, 1), (second, -1)):
        along, against = shift(block, "x", way), shift(block, "x", -way)
        own.append([block, along, against, shift(against, "x", -way)])
        other.append(swap(block, "zh", 1))
    other[0], own[0], own[1][1:] = lax.optimization_barrier((other[0], own[0], own[1][1:]))
    chunks = []
    for n, way in ((0, 1), (1, -1)):
        along, against = shift(other[n], "x", way), shift(other[n], "x", -way)
        others = [other[n], along, against, shift(along, "x", way)]
        order = (0, 1, 2, 3) if way > 0 else (0, 2, 1, 3)
        chunks.append([kind[k] for k in order for kind in (own[n], others)])
    return chunks


def choose(index, options):
    value = options[3]
    for k in (2, 1, 0):
        value = jnp.where(index == k, options[k], value)
    return value


def pack_y(place, merged, tag, send):
    features, half = send.shape[0] - 8, send.shape[1]
    quarter = features // 4
    packet = shape((quarter + STEP, half), BF16)
    outs = (shape((quarter, half), F32), packet, packet, packet, shape((8, 128), F32))
    return call(pack_y_kernel, "pack_y", place, (merged, tag, swap(send, "c", 1)), outs)


def over_y(packed):
    return [shift(p, "y", k) for k, p in enumerate(packed[1:4], 1)]


def sum_over_replicas(place, packed, got, after):
    own, scale = packed[0], packed[4]
    quarter, half = own.shape
    small = half // 4
    y, zl = place[0], place[1]
    tag = shape((8, 128), F32)
    packet = shape((quarter + STEP, small), BF16)
    mine, q1, q2, q3, scale = call(
        turn_kernel, "turn", place, (own, scale, *got),
        (shape((quarter, small), F32), packet, packet, packet, tag),
        (pltpu.VMEM((quarter, half), F32),), after=after,
    )
    r1, r2, r3 = (swap(q, "zl", k) for k, q in ((1, q1), (2, q2), (3, q3)))
    code, scale = call(
        finish_kernel, "finish", place, (mine, scale, r1, r2, r3), (shape((quarter, small), BF16), tag)
    )
    pieces = [code] + [swap(code, "zl", k) for k in (1, 2, 3)]
    line = jnp.concatenate([choose(zl, [pieces[j ^ k] for k in range(4)]) for j in range(4)], axis=1)
    lines = [line] + [shift(line, "y", k) for k in (1, 2, 3)]
    mine = jnp.concatenate([choose(y, [lines[(k - j) % 4] for k in range(4)]) for j in range(4)], axis=0)
    return mine, swap(mine, "c", 1), scale


def on_device(replicas, x_ctx, d_out, weight, error, q_init):
    place = jnp.stack([lax.axis_index(name) for name in ("y", "zl", "c", "x", "zh")]).astype(jnp.int32)
    columns = d_out.shape[1]
    features = x_ctx.shape[1]
    rank = q_init.shape[0]
    third = columns // 3
    xt = x_ctx.T
    error = error[0]
    chunks = [slice(a * third, (a + n) * third) for a, n in THIRDS]
    tokens = gather_tokens(*[d_out[:, cols] for cols in chunks])
    merged, packed, got = [], [], []
    for n, (cols, blocks) in enumerate(zip(chunks, tokens)):
        width = cols.stop - cols.start
        later = tokens[n + 1] if n + 1 < len(tokens) else ()
        values, send, tag = call(
            functools.partial(merge_kernel, cols.start), "merge", place, (xt, error, *blocks),
            (shape((features, width), F32), shape((features + 8, width // 2), F32), shape((8, 128), F32)),
            (pltpu.VMEM(xt.shape, BF16), pltpu.VMEM((STEP, width // 2), F32)), 2 * xt.size * width,
            [later[5]] if later else [got[n - 1][0]],
        )
        merged.append(values)
        packed.append(pack_y(place, values, tag, send))
        got.append(over_y(packed[-1]))
    (d_input,) = call(
        input_kernel, "d_input", place, (weight, *sum(tokens, [])), (shape(x_ctx.shape, BF16),),
        (pltpu.VMEM(x_ctx.shape, F32),), 2 * x_ctx.size * columns, [packed[-1][1]],
    )
    earlier, products = [], ()
    for n, cols in enumerate(chunks):
        last = n + 1 == len(chunks)
        sums = sum_over_replicas(place, packed[n], got[n], [d_input] if last else [packed[n + 1][1]])
        if last:
            break
        wide = shape((features, cols.stop - cols.start), BF16)
        high, low, total = call(
            functools.partial(first_kernel, cols.start), "first", place, (*sums, q_init, *products),
            (wide, wide, shape((rank + features, features), F32)),
        )
        products = (total,)
        earlier += [high, low, merged[n]]
    wide = pltpu.VMEM(merged[-1].shape, BF16)
    left, right, new_error = call(
        functools.partial(last_kernel, replicas), "last", place,
        (*sums, q_init, *products, *earlier, merged[-1]),
        (shape((rank, features), F32), shape((rank, columns), F32), shape((features, columns), BF16)),
        (wide, wide),
    )
    return d_input, new_error[None], left, right


def solution(mesh):
    names = ("y", "zl", "c", "x", "zh")
    fine = Mesh(mesh.devices.reshape([SIZES[name] for name in names]), names)
    return jax.shard_map(
        functools.partial(on_device, mesh.shape["dp"]),
        mesh=fine,
        in_specs=(
            P(DP, TENSOR),
            P(DP + TENSOR, None),
            P(TENSOR, None),
            P(DP, TENSOR, None),
            P(None, TENSOR),
        ),
        out_specs=(
            P(DP, TENSOR),
            P(DP, TENSOR, None),
            P(None, TENSOR),
            P(None, TENSOR),
        ),
        check_vma=False,
    )
```

```python
import functools
import math

import jax
import jax.numpy as jnp
from jax import lax
from jax.experimental import pallas as pl
from jax.experimental.pallas import tpu as pltpu
from jax.sharding import Mesh, PartitionSpec as P

ITERS = 3
EPSILON = 1e-06
DP = ("y", "zl", "c")
TENSOR = ("x", "zh")
SIZES = {"y": 4, "zl": 4, "c": 2, "x": 4, "zh": 2}
THIRDS = ((0, 2), (2, 1))
CONTRACT_LAST = (((1,), (1,)), ((), ()))
CONTRACT_FIRST = (((0,), (0,)), ((), ()))
LIMIT = 56 * 1024 * 1024
F32, BF16 = jnp.float32, jnp.bfloat16
STEP = 16

RATIO = 512.0
POWER = 250.0 / math.log2(RATIO + math.sqrt(RATIO * RATIO + 1.0))


def encode(value, scale):
    t = jnp.abs(value) * (RATIO / scale)
    code = jnp.exp2(POWER * jnp.log2(t + jnp.sqrt(t * t + 1.0)) - 125.0)
    return jnp.where(value < 0, -code, code).astype(BF16)


def decode(code, scale):
    code = code.astype(F32)
    t = jnp.exp2((jnp.log2(jnp.abs(code)) + 125.0) * (1.0 / POWER))
    value = (t - 1.0 / t) * (scale * (0.5 / RATIO))
    return jnp.where(code < 0, -value, value)


def split(value):
    high = value.astype(BF16)
    return high, (value - high.astype(F32)).astype(BF16)


def shift(value, axis, by):
    n = SIZES[axis]
    return lax.ppermute(value, axis, [(i, (i + by) % n) for i in range(n)])


def swap(value, axis, by):
    return lax.ppermute(value, axis, [(i, i ^ by) for i in range(SIZES[axis])])


def whole(*arrays):
    return [pl.BlockSpec(memory_space=pltpu.VMEM) for _ in arrays]


def call(kernel, name, place, arrays, outs, scratch=(), after=(), grid=(), in_specs=None, out_specs=None):
    def body(place_ref, *refs):
        kernel(place_ref, *refs[len(after) :])

    return pl.pallas_call(
        body,
        grid=grid,
        out_shape=tuple(outs),
        in_specs=[pl.BlockSpec(memory_space=pltpu.SMEM)]
        + [pl.BlockSpec(memory_space=pl.ANY)] * len(after)
        + (in_specs or whole(*arrays)),
        out_specs=tuple(out_specs or whole(*outs)),
        scratch_shapes=list(scratch),
        compiler_params=pltpu.CompilerParams(vmem_limit_bytes=LIMIT),
        cost_estimate=pl.CostEstimate(flops=0, bytes_accessed=0, transcendentals=0),
        name=name,
    )(place, *after, *arrays)


def shape(dims, dtype):
    return jax.ShapeDtypeStruct(dims, dtype)


def steps(rows, body):
    @pl.loop(0, rows // STEP)
    def _(i):
        body(pl.ds(pl.multiple_of(i * STEP, STEP), STEP), i)


def rows_at(start, i):
    return pl.ds(pl.multiple_of(start + i * STEP, STEP), STEP)


def block_order(place_ref):
    x, zh = place_ref[3], place_ref[4]
    order = []
    for by in (0, 3, 1, 2):
        at = lax.rem(x + by, 4) * 2
        order += [at + zh, at + 1 - zh]
    return order


def merge_kernel(place_ref, xt_ref, error_ref, *refs):
    blocks, (merged_ref, send_ref, tag_ref, x_ref, top_ref) = refs[:8], refs[8:]
    rows, tile = blocks[0].shape
    features, half = send_ref.shape[0] - 8, send_ref.shape[1]
    k, c = pl.program_id(0), place_ref[2]

    @pl.when(k == 0)
    def _():
        for b, at in enumerate(block_order(place_ref)):
            x_ref[:, b * rows : (b + 1) * rows] = xt_ref[:, pl.ds(pl.multiple_of(at * rows, rows), rows)]
        top_ref[...] = jnp.zeros_like(top_ref)

    tokens = jnp.concatenate([ref[...] for ref in blocks], axis=0)
    grad = jnp.dot(x_ref[...], tokens, preferred_element_type=F32)
    merged_ref[...] = grad + error_ref[...].astype(F32)

    def body(at, _):
        top_ref[...] = jnp.maximum(top_ref[...], jnp.abs(merged_ref[at, :]))

    steps(features, body)
    each = half // tile

    @pl.when(k // each == 1 - c)
    def _():
        send_ref[:features, pl.ds(pl.multiple_of(lax.rem(k, each) * tile, tile), tile)] = merged_ref[...]

    @pl.when(k == 2 * each - 1)
    def _():
        top = jnp.max(jnp.max(top_ref[...], axis=0, keepdims=True), axis=1, keepdims=True)
        send_ref[features:, :] = jnp.broadcast_to(top, (8, half))
        tag_ref[...] = jnp.broadcast_to(top, tag_ref.shape)


def merge(place, xt, error, blocks, base, after):
    rows, width = blocks[0].shape
    features, tokens = xt.shape
    half = width // 2
    tile = min(512, half)
    first = base // tile
    outs = (shape((features, width), F32), shape((features + 8, half), F32), shape((8, 128), F32))
    return call(
        merge_kernel, "merge", place, (xt, error, *blocks), outs,
        (pltpu.VMEM((features, tokens), BF16), pltpu.VMEM((STEP, tile), F32)), after, (width // tile,),
        [pl.BlockSpec((features, tokens), lambda k: (0, 0)), pl.BlockSpec((features, tile), lambda k: (0, first + k))]
        + [pl.BlockSpec((rows, tile), lambda k: (0, k))] * 8,
        [pl.BlockSpec((features, tile), lambda k: (0, k)), pl.BlockSpec((features + 8, half), lambda k: (0, 0)),
         pl.BlockSpec((8, 128), lambda k: (0, 0))],
    )


def pack_y_kernel(place_ref, merged_ref, tag_ref, got_ref, own_ref, p1_ref, p2_ref, p3_ref, scale_ref):
    y, c = place_ref[0], place_ref[2]
    quarter, half = own_ref.shape
    features = 4 * quarter
    here = pl.multiple_of(c * half, half)
    top = jnp.maximum(tag_ref[0:1, 0:1], got_ref[features:, :][0:1, 0:1])
    scale = jnp.maximum(top * 2.008, 1e-30).astype(BF16).astype(F32)
    scale_ref[...] = jnp.broadcast_to(scale, scale_ref.shape)
    starts = [lax.rem(y + k, 4) * quarter for k in range(4)]

    def total(start, i):
        rows = rows_at(start, i)
        return merged_ref[rows, pl.ds(here, half)] + got_ref[rows, :]

    def pack(rows, i):
        own_ref[rows, :] = total(starts[0], i)
        for k, ref in ((1, p1_ref), (2, p2_ref), (3, p3_ref)):
            ref[rows, :] = encode(total(starts[k], i), scale)

    steps(quarter, pack)
    for ref in (p1_ref, p2_ref, p3_ref):
        ref[quarter:, :] = jnp.broadcast_to(scale, (STEP, half)).astype(BF16)


def scale_of(ref, rows):
    return ref[rows:, :][0:1, 0:1].astype(F32)


def turn_kernel(place_ref, own_ref, scale_ref, r1_ref, r2_ref, r3_ref, mine_ref, q1_ref, q2_ref, q3_ref, next_ref, part_ref):
    zl = place_ref[1]
    quarter, half = own_ref.shape
    small = half // 4
    got = (r1_ref, r2_ref, r3_ref)
    scales = [scale_of(ref, quarter) for ref in got]
    scale = scale_ref[0:1, 0:1]
    for other in scales:
        scale = jnp.maximum(scale, other)
    scale = scale * 4.0
    next_ref[...] = jnp.broadcast_to(scale, next_ref.shape)

    def body(rows, _):
        part = own_ref[rows, :]
        for ref, other in zip(got, scales):
            part = part + decode(ref[rows, :], other)
        part_ref[rows, :] = part

    steps(quarter, body)

    def piece(rows, k):
        at = lax.bitwise_xor(zl, k) * small
        return part_ref[rows, pl.ds(pl.multiple_of(at, small), small)]

    def pack(rows, _):
        mine_ref[rows, :] = piece(rows, 0)
        for k, ref in ((1, q1_ref), (2, q2_ref), (3, q3_ref)):
            ref[rows, :] = encode(piece(rows, k), scale)

    steps(quarter, pack)
    for ref in (q1_ref, q2_ref, q3_ref):
        ref[quarter:, :] = jnp.broadcast_to(scale, (STEP, small)).astype(BF16)


def finish_kernel(place_ref, mine_ref, scale_ref, r1_ref, r2_ref, r3_ref, code_ref, last_ref):
    quarter, _ = mine_ref.shape
    got = (r1_ref, r2_ref, r3_ref)
    scales = [scale_of(ref, quarter) for ref in got]
    scale = scale_ref[0:1, 0:1]
    for other in scales:
        scale = jnp.maximum(scale, other)
    scale = scale * 4.0
    last_ref[...] = jnp.broadcast_to(scale, last_ref.shape)

    def body(rows, _):
        total = mine_ref[rows, :]
        for ref, other in zip(got, scales):
            total = total + decode(ref[rows, :], other)
        code_ref[rows, :] = encode(total, scale)

    steps(quarter, body)


def unpack(place_ref, own_ref, other_ref, scale_ref, high_ref, low_ref):
    c = place_ref[2]
    features, half = own_ref.shape
    scale = scale_ref[0:1, 0:1]

    def body(rows, _):
        for ref, at in ((own_ref, c), (other_ref, 1 - c)):
            high, low = split(decode(ref[rows, :], scale))
            cols = pl.ds(pl.multiple_of(at * half, half), half)
            high_ref[rows, cols] = high
            low_ref[rows, cols] = low

    steps(features, body)


def gram(start, high, low):
    start_high, start_low = split(start)
    rows_high = jnp.concatenate([start_high, high], axis=0)
    rows_low = jnp.concatenate([start_low, low], axis=0)
    total = lax.dot_general(rows_high, high, CONTRACT_LAST, preferred_element_type=F32)
    total = total + lax.dot_general(rows_high, low, CONTRACT_LAST, preferred_element_type=F32)
    return total + lax.dot_general(rows_low, high, CONTRACT_LAST, preferred_element_type=F32)


def first_kernel(base, place_ref, own_ref, other_ref, scale_ref, start_ref, *refs):
    *before, high_ref, low_ref, gram_ref = refs
    unpack(place_ref, own_ref, other_ref, scale_ref, high_ref, low_ref)
    width = high_ref.shape[1]
    products = gram(start_ref[:, base : base + width], high_ref[...], low_ref[...])
    for ref in before:
        products = products + ref[...]
    gram_ref[...] = products


def orthonormal(matrix):
    taken = jnp.zeros_like(matrix)
    rows = []
    for j in range(matrix.shape[0]):
        row = matrix[j : j + 1, :] - taken[j : j + 1, :]
        scale = lax.rsqrt(jnp.sum(row * row, axis=1, keepdims=True) + EPSILON)
        along = jnp.sum(matrix * row, axis=1, keepdims=True) * scale
        row = row * scale
        rows.append(row)
        taken = taken + along * row
    return jnp.concatenate(rows, axis=0)


def times(left, high, low):
    rank = left.shape[0]
    left_high, left_low = split(left)
    both = jnp.dot(jnp.concatenate([left_high, left_low], axis=0), high, preferred_element_type=F32)
    return both[:rank] + both[rank:] + jnp.dot(left_high, low, preferred_element_type=F32)


def last_kernel(replicas, place_ref, own_ref, other_ref, scale_ref, start_ref, products_ref, *refs):
    *earlier, merged_ref, left_ref, right_ref, error_ref, high_ref, low_ref = refs
    parts = [tuple(earlier[i : i + 3]) for i in range(0, len(earlier), 3)] + [(high_ref, low_ref, merged_ref)]
    rank, columns = right_ref.shape
    width = merged_ref.shape[1]
    unpack(place_ref, own_ref, other_ref, scale_ref, high_ref, low_ref)
    products = products_ref[...] + gram(start_ref[:, columns - width :], high_ref[...], low_ref[...])
    left = orthonormal(products[:rank])
    gram_high, gram_low = split(products[rank:])
    for _ in range(ITERS - 1):
        left = orthonormal(times(left, gram_high, gram_low) * (1.0 / replicas))
    left_ref[...] = left
    left_high, left_low = split(left)
    left_parts = jnp.concatenate([left_high, left_high, left_low], axis=0)
    base = 0
    for hi_ref, lo_ref, merged in parts:
        width = merged.shape[1]
        tile = min(width, 512)
        for k in range(width // tile):
            cols = slice(k * tile, (k + 1) * tile)
            out = slice(base + k * tile, base + (k + 1) * tile)
            right = times(left, hi_ref[:, cols], lo_ref[:, cols]) * (1.0 / replicas)
            right_ref[:, out] = right
            right_high, right_low = split(right)
            right_parts = jnp.concatenate([right_high, right_low, right_high], axis=0)
            approx = lax.dot_general(left_parts, right_parts, CONTRACT_FIRST, preferred_element_type=F32)
            error_ref[:, out] = (merged[:, cols] - approx).astype(BF16)
        base += width


def input_kernel(split_at, place_ref, weight_ref, *refs):
    *blocks, out_ref, acc_ref = refs
    rows = blocks[0].shape[0]
    k = pl.program_id(0)

    def add(chunk):
        tokens = jnp.concatenate([ref[...] for ref in chunk], axis=0)
        acc_ref[...] += lax.dot_general(tokens, weight_ref[...], CONTRACT_LAST, preferred_element_type=F32)

    @pl.when(k == 0)
    def _():
        acc_ref[...] = jnp.zeros_like(acc_ref)

    @pl.when(k < split_at)
    def _():
        add(blocks[:8])

    @pl.when(k >= split_at)
    def _():
        add(blocks[8:])

    @pl.when(k == pl.num_programs(0) - 1)
    def _():
        for b, at in enumerate(block_order(place_ref)):
            here = pl.ds(pl.multiple_of(at * rows, rows), rows)
            out_ref[here, :] = acc_ref[b * rows : (b + 1) * rows, :].astype(BF16)


def project(place, weight, first, second, dims, after):
    rows = first[0].shape[0]
    features, columns = weight.shape
    tile = min(512, second[0].shape[1] // 2)
    n = first[0].shape[1] // tile
    return call(
        functools.partial(input_kernel, n), "d_input", place, (weight, *first, *second), (shape(dims, BF16),),
        (pltpu.VMEM(dims, F32),), after, (columns // tile,),
        [pl.BlockSpec((features, tile), lambda k: (0, k))]
        + [pl.BlockSpec((rows, tile), lambda k: (0, jnp.minimum(k, n - 1)))] * 8
        + [pl.BlockSpec((rows, tile), lambda k: (0, jnp.maximum(k - n, 0)))] * 8,
        [pl.BlockSpec(dims, lambda k: (0, 0))],
    )[0]


def gather_tokens(first, second):
    own, other = [], []
    for block, way in ((first, 1), (second, -1)):
        along, against = shift(block, "x", way), shift(block, "x", -way)
        own.append([block, along, against, shift(against, "x", -way)])
        other.append(swap(block, "zh", 1))
    other[0], own[0], own[1][1:] = lax.optimization_barrier((other[0], own[0], own[1][1:]))
    chunks = []
    for n, way in ((0, 1), (1, -1)):
        along, against = shift(other[n], "x", way), shift(other[n], "x", -way)
        others = [other[n], along, against, shift(along, "x", way)]
        order = (0, 1, 2, 3) if way > 0 else (0, 2, 1, 3)
        chunks.append([kind[k] for k in order for kind in (own[n], others)])
    return chunks


def choose(index, options):
    value = options[3]
    for k in (2, 1, 0):
        value = jnp.where(index == k, options[k], value)
    return value


def pack_y(place, merged, tag, send):
    features, half = send.shape[0] - 8, send.shape[1]
    quarter = features // 4
    packet = shape((quarter + STEP, half), BF16)
    outs = (shape((quarter, half), F32), packet, packet, packet, shape((8, 128), F32))
    return call(pack_y_kernel, "pack_y", place, (merged, tag, swap(send, "c", 1)), outs)


def over_y(packed):
    return [shift(p, "y", k) for k, p in enumerate(packed[1:4], 1)]


def sum_over_replicas(place, packed, got, after):
    own, scale = packed[0], packed[4]
    quarter, half = own.shape
    small = half // 4
    y, zl = place[0], place[1]
    tag = shape((8, 128), F32)
    packet = shape((quarter + STEP, small), BF16)
    mine, q1, q2, q3, scale = call(
        turn_kernel, "turn", place, (own, scale, *got),
        (shape((quarter, small), F32), packet, packet, packet, tag),
        (pltpu.VMEM((quarter, half), F32),), after=after,
    )
    r1, r2, r3 = (swap(q, "zl", k) for k, q in ((1, q1), (2, q2), (3, q3)))
    code, scale = call(
        finish_kernel, "finish", place, (mine, scale, r1, r2, r3), (shape((quarter, small), BF16), tag)
    )
    pieces = [code] + [swap(code, "zl", k) for k in (1, 2, 3)]
    line = jnp.concatenate([choose(zl, [pieces[j ^ k] for k in range(4)]) for j in range(4)], axis=1)
    lines = [line] + [shift(line, "y", k) for k in (1, 2, 3)]
    mine = jnp.concatenate([choose(y, [lines[(k - j) % 4] for k in range(4)]) for j in range(4)], axis=0)
    return mine, swap(mine, "c", 1), scale


def on_device(replicas, x_ctx, d_out, weight, error, q_init):
    place = jnp.stack([lax.axis_index(name) for name in ("y", "zl", "c", "x", "zh")]).astype(jnp.int32)
    columns = d_out.shape[1]
    features = x_ctx.shape[1]
    rank = q_init.shape[0]
    third = columns // 3
    xt = x_ctx.T
    error = error[0]
    chunks = [slice(a * third, (a + n) * third) for a, n in THIRDS]
    tokens = gather_tokens(*[d_out[:, cols] for cols in chunks])
    merged, packed, got = [], [], []
    for n, (cols, blocks) in enumerate(zip(chunks, tokens)):
        later = tokens[n + 1] if n + 1 < len(tokens) else ()
        values, send, tag = merge(place, xt, error, blocks, cols.start, [later[5]] if later else [got[n - 1][0]])
        merged.append(values)
        packed.append(pack_y(place, values, tag, send))
        got.append(over_y(packed[-1]))
    d_input = project(place, weight, *tokens, x_ctx.shape, [packed[-1][1]])
    earlier, products = [], ()
    for n, cols in enumerate(chunks):
        last = n + 1 == len(chunks)
        sums = sum_over_replicas(place, packed[n], got[n], [d_input] if last else [packed[n + 1][1]])
        if last:
            break
        wide = shape((features, cols.stop - cols.start), BF16)
        high, low, total = call(
            functools.partial(first_kernel, cols.start), "first", place, (*sums, q_init, *products),
            (wide, wide, shape((rank + features, features), F32)),
        )
        products = (total,)
        earlier += [high, low, merged[n]]
    wide = pltpu.VMEM(merged[-1].shape, BF16)
    left, right, new_error = call(
        functools.partial(last_kernel, replicas), "last", place,
        (*sums, q_init, *products, *earlier, merged[-1]),
        (shape((rank, features), F32), shape((rank, columns), F32), shape((features, columns), BF16)),
        (wide, wide),
    )
    return d_input, new_error[None], left, right


def solution(mesh):
    names = ("y", "zl", "c", "x", "zh")
    fine = Mesh(mesh.devices.reshape([SIZES[name] for name in names]), names)
    return jax.shard_map(
        functools.partial(on_device, mesh.shape["dp"]),
        mesh=fine,
        in_specs=(
            P(DP, TENSOR),
            P(DP + TENSOR, None),
            P(TENSOR, None),
            P(DP, TENSOR, None),
            P(None, TENSOR),
        ),
        out_specs=(
            P(DP, TENSOR),
            P(DP, TENSOR, None),
            P(None, TENSOR),
            P(None, TENSOR),
        ),
        check_vma=False,
    )
```
